256 devices in a mesh: tup: 32 (over z, y), lang: 8 (over x, core).
Axes of the slice: x: 4, y: 4, z: 8, core: 2. Of those that a mesh axis runs over, the one named last changes fastest.
Arguments:
- counts: bfloat16 [8, 4096, 16384], P('lang', 'tup'), may hold values from 0 to 80
- lengths: int32 [8, 4096], P('lang', 'tup'), may hold values from 96 to 128, as said below
- tuple_map: int32 [8, 4096], P('lang', 'tup'), may hold values from 0 to 4095, as said below
- topic_mix: bfloat16 [4096, 256], P('tup'), may hold values from 0.049804688 to 5
- word_probs: bfloat16 [8, 16384, 256], P('lang', 'tup'), may hold values from 0.099609375 to 10
Outputs:
- mix_update: float32 [4096, 256], P('tup')
- word_update: float32 [8, 16384, 256], P('lang', 'tup')
The draws below stay inside these ranges and needn't reach their ends.
Inputs may be any that keep to these rules, and one draw needn't show every extreme that they name: `lengths`: the first row of every language spans all 128 tiles. `tuple_map`: each language names every tuple once; the 128 rows of one index of tup hold exactly 4 tuples t of each value of t // 128.
All inputs are finite; a program needn't handle non-finite values.
Results may differ from the reference program's by a relative error of at most 0.0003.
Values may be sent and summed in bfloat16 or wider, within the bound.
No kernel may reach another device: no remote copies, remote signals or barrier semaphores. Data moves between devices by JAX's collectives and lax.ppermute only.
A program may use at most 128 MiB of HBM per device.

```python
import math
import jax
import jax.numpy as jnp
from jax import lax

VOCAB = 16384
TOPICS = 256
TUP_DEV = 128
LANGS = 8
TUPLES = 4096
TILES = 128


def draw_counts(key, part):
    shape_all = (LANGS, TUPLES, VOCAB)
    values = jnp.exp(jax.random.uniform(jax.random.fold_in(key, 12), shape_all, minval=jnp.log(0.25), maxval=jnp.log(8.0)))
    return values.astype(jnp.bfloat16)


def draw_lengths(key, part):
    lowest = max(3 * TILES // 4, 1)
    result = jax.random.randint(jax.random.fold_in(key, 21), (LANGS, TUPLES), lowest, TILES + 1)
    result = result.at[:, 0].set(TILES)
    result = result.at[:, 1].set(lowest)
    return result.astype(jnp.int32)


def draw_tuple_map(key, part):
    owners = TUPLES // TUP_DEV
    per_owner = TUP_DEV // owners
    key_list = jax.random.split(jax.random.fold_in(key, 31), LANGS * owners)
    slot_rows = jax.vmap(lambda subkey: jax.random.permutation(subkey, TUP_DEV))(key_list)
    slot_rows = slot_rows.reshape(LANGS, owners, owners, per_owner)
    tuple_ids = slot_rows + (jnp.arange(owners, dtype=jnp.int32) * TUP_DEV)[None, :, None, None]
    tuple_ids = jnp.transpose(tuple_ids, (0, 2, 1, 3)).reshape(LANGS, owners, TUP_DEV)
    other_keys = jax.random.split(jax.random.fold_in(key, 32), LANGS * owners)
    shuffle = jax.vmap(lambda subkey: jax.random.permutation(subkey, TUP_DEV))(other_keys).reshape(LANGS, owners, TUP_DEV)
    tuple_ids = jnp.take_along_axis(tuple_ids, shuffle, axis=2)
    return tuple_ids.reshape(LANGS, TUPLES).astype(jnp.int32)


def level_of(own_key, extent, shards, smallest, top_value):
    factor_of = 1.0
    for position, parts in shards:
        heights = jax.random.uniform(jax.random.fold_in(jax.random.fold_in(own_key, 6), position), (parts,), jnp.float32, smallest / len(shards), top_value / len(shards))
        factor_of = factor_of * jnp.repeat(jnp.exp(heights), extent[position] // parts).reshape((-1,) + (1,) * (len(extent) - 1 - position))
    return factor_of


def setup_inputs(seed: int = 0) -> dict:
    keys = jax.random.split(jax.random.key(seed), 6)
    return {
        "counts": draw_counts(jax.random.fold_in(keys[5], 71), 0),
        "lengths": draw_lengths(jax.random.fold_in(keys[5], 71), 0),
        "tuple_map": draw_tuple_map(jax.random.fold_in(keys[5], 71), 0),
        "topic_mix": jnp.clip(jnp.exp(math.log(5.0) - 4.609084 * jax.random.uniform(keys[3], (TUPLES, TOPICS), jnp.float32) ** level_of(keys[3], (TUPLES, TOPICS), ((0, 32),), -0.2, 0.2)), 0.049804688, 5.0).astype(jnp.bfloat16),
        "word_probs": jnp.clip(jnp.exp(math.log(10.0) - 4.609084 * jax.random.uniform(keys[4], (LANGS, VOCAB, TOPICS), jnp.float32) ** level_of(keys[4], (LANGS, VOCAB, TOPICS), ((0, 8), (1, 32)), -0.2, 0.2)), 0.099609375, 10.0).astype(jnp.bfloat16),
    }


def ratio_block(count_block, mix_block, word_block):
    expected = lax.dot_general(mix_block, word_block, (((1,), (1,)), ((), ())), preferred_element_type=jnp.float32)
    return count_block.astype(jnp.float32) / expected


def reference(counts, lengths, tuple_map, topic_mix, word_probs):
    tile_of = jnp.arange(VOCAB, dtype=jnp.int32) // 128
    block_rows = math.gcd(TUPLES, 512)

    def one_language(inputs):
        count_rows, length_rows, tuple_ids, word_rows = inputs
        live_counts = count_rows * (tile_of[None, :] < length_rows[:, None]).astype(jnp.bfloat16)
        mix_rows = topic_mix[tuple_ids]
        word_wide = word_rows.astype(jnp.float32)

        def step_block(word_total, block_in):
            live_block, mix_block = block_in
            ratios = ratio_block(live_block, mix_block, word_rows)
            topic_block = jnp.dot(ratios, word_wide, precision=lax.Precision.HIGHEST)
            word_total = word_total + lax.dot_general(ratios, mix_block.astype(jnp.float32), (((0,), (0,)), ((), ())), precision=lax.Precision.HIGHEST)
            return word_total, topic_block

        word_total, topic_blocks = lax.scan(
            step_block,
            jnp.zeros((VOCAB, TOPICS), jnp.float32),
            (live_counts.reshape(-1, block_rows, VOCAB), mix_rows.reshape(-1, block_rows, TOPICS)))
        topic_total = jnp.zeros((TUPLES, TOPICS), jnp.float32).at[tuple_ids].set(topic_blocks.reshape(TUPLES, TOPICS))
        return topic_total, word_total

    topic_totals, word_totals = lax.map(one_language, (counts, lengths, tuple_map, word_probs))
    mixed = topic_mix.astype(jnp.float32) * jnp.sum(topic_totals, 0)
    mix_update = TOPICS * mixed / jnp.sum(mixed, 1, keepdims=True)
    scaled = word_probs.astype(jnp.float32) * word_totals
    word_update = VOCAB * scaled / jnp.sum(scaled, 1, keepdims=True)
    return mix_update, word_update
```

```python
import functools

import jax
import jax.numpy as jnp
from jax import lax
from jax.experimental import pallas as pl
from jax.experimental.pallas import tpu as pltpu
from jax.sharding import Mesh
from jax.sharding import PartitionSpec as P

ZS, YS, XS, CS = 8, 4, 4, 2
TUP = ZS * YS
LANG = XS * CS
ROWS = 128
TOPICS = 256
SHARD = 512
VOCAB = 16384
LANES = 128
CHUNKS = (256, 256)
GROUP = YS * ROWS
EACH = ROWS // TUP
HALF = jnp.bfloat16
FULL = jnp.float32


def split_kernel(y_ref, len_ref, count_ref, *out_refs):
    block = pl.program_id(0)
    here = y_ref[0]
    spans = len_ref[...]
    per = SHARD // LANES
    for s in range(YS):
        there = lax.rem(here + s, YS)
        begin = pl.multiple_of(there * SHARD, SHARD)
        at = 0
        for c, width in enumerate(CHUNKS):
            for q in range(width // LANES):
                tile = (block * YS + there) * per + at // LANES
                keep = (tile < spans).astype(FULL).astype(HALF)
                part = count_ref[:, pl.ds(pl.multiple_of(begin + at, LANES), LANES)]
                out_refs[c * YS + s][:, q * LANES : (q + 1) * LANES] = part * keep
                at += LANES


def split_counts(count_rows, lengths, here):
    shapes, specs = [], []
    for width in CHUNKS:
        for _ in range(YS):
            shapes.append(jax.ShapeDtypeStruct((ROWS, ZS * width), HALF))
            specs.append(pl.BlockSpec((ROWS, width), lambda i, y: (0, i)))
    return pl.pallas_call(
        split_kernel,
        grid_spec=pltpu.PrefetchScalarGridSpec(
            num_scalar_prefetch=1,
            grid=(ZS,),
            in_specs=[
                pl.BlockSpec((ROWS, 1), lambda i, y: (0, 0)),
                pl.BlockSpec((ROWS, YS * SHARD), lambda i, y: (0, i)),
            ],
            out_specs=specs,
        ),
        out_shape=shapes,
        compiler_params=pltpu.CompilerParams(vmem_limit_bytes=24 * 2**20),
        cost_estimate=pl.CostEstimate(flops=2**21, bytes_accessed=2**23, transcendentals=0),
        name="split_counts",
    )(here, lengths, count_rows)


def ratio_kernel(*refs):
    count_refs = refs[:YS]
    mix_ref, turned_ref, word_ref, before_ref, topic_ref, word_out = refs[YS:]

    @pl.when(pl.program_id(0) == 0)
    def _():
        topic_ref[...] = before_ref[...]

    words = word_ref[0]
    counts = jnp.concatenate([r[...] for r in count_refs], axis=0)
    expected = lax.dot_general(
        mix_ref[...], words, (((1,), (1,)), ((), ())), preferred_element_type=FULL
    )
    ratios = counts.astype(FULL) / expected
    high = ratios.astype(HALF)
    low = (ratios - high.astype(FULL)).astype(HALF)
    topic_ref[...] += jnp.dot(high, words, preferred_element_type=FULL) + jnp.dot(
        low, words, preferred_element_type=FULL
    )
    turned = turned_ref[...]
    word_out[0] = jnp.dot(turned, high, preferred_element_type=FULL) + jnp.dot(
        turned, low, preferred_element_type=FULL
    )


def ratio_pass(parts, mix, turned, words, before, width):
    return pl.pallas_call(
        ratio_kernel,
        grid=(ZS,),
        in_specs=[pl.BlockSpec((ROWS, width), lambda i: (0, i))] * YS
        + [
            pl.BlockSpec((GROUP, TOPICS), lambda i: (0, 0)),
            pl.BlockSpec((TOPICS, GROUP), lambda i: (0, 0)),
            pl.BlockSpec((1, width, TOPICS), lambda i: (i, 0, 0)),
            pl.BlockSpec((GROUP, TOPICS), lambda i: (0, 0)),
        ],
        out_specs=[
            pl.BlockSpec((GROUP, TOPICS), lambda i: (0, 0)),
            pl.BlockSpec((1, TOPICS, width), lambda i: (i, 0, 0)),
        ],
        out_shape=[
            jax.ShapeDtypeStruct((GROUP, TOPICS), FULL),
            jax.ShapeDtypeStruct((ZS, TOPICS, width), FULL),
        ],
        compiler_params=pltpu.CompilerParams(vmem_limit_bytes=32 * 2**20),
        cost_estimate=pl.CostEstimate(
            flops=10 * GROUP * ZS * width * TOPICS,
            bytes_accessed=ZS * width * (2 * GROUP + 6 * TOPICS),
            transcendentals=GROUP * ZS * width,
        ),
        name="ratio_pass",
    )(*parts, mix, turned, words, before)


def exact_select(chosen, values):
    total = None
    rest = values
    for _ in range(3):
        piece = rest.astype(HALF)
        rest = rest - piece.astype(FULL)
        term = jnp.dot(chosen, piece, preferred_element_type=FULL)
        total = term if total is None else total + term
    return total


def fetch_kernel(slot_ref, arrived_ref, mix_ref, turned_ref):
    spots = lax.broadcasted_iota(jnp.int32, (GROUP, GROUP), 1)
    chosen = (slot_ref[...] == spots).astype(FULL).astype(HALF)
    mix = jnp.dot(chosen, arrived_ref[...], preferred_element_type=FULL)
    mix_ref[...] = mix.astype(HALF)
    turned_ref[...] = mix.T.astype(HALF)


def fetch_mix(slots, arrived):
    return pl.pallas_call(
        fetch_kernel,
        out_shape=[
            jax.ShapeDtypeStruct((GROUP, TOPICS), HALF),
            jax.ShapeDtypeStruct((TOPICS, GROUP), HALF),
        ],
        compiler_params=pltpu.CompilerParams(vmem_limit_bytes=24 * 2**20),
        name="fetch_mix",
    )(slots.reshape(GROUP, 1), arrived)


def give_kernel(ask_ref, topic_ref, out_ref):
    spots = lax.broadcasted_iota(jnp.int32, (GROUP, ROWS), 1)
    chosen = (ask_ref[...] == spots).astype(FULL).astype(HALF)
    out_ref[...] = jnp.dot(chosen, topic_ref[...], preferred_element_type=FULL).astype(HALF)


def give_mix(asked, topic_mix):
    return pl.pallas_call(
        give_kernel,
        out_shape=jax.ShapeDtypeStruct((GROUP, TOPICS), HALF),
        compiler_params=pltpu.CompilerParams(vmem_limit_bytes=24 * 2**20),
        name="give_mix",
    )(asked.reshape(GROUP, 1), topic_mix)


def pack_kernel(slot_ref, topic_ref, mix_ref, out_ref, column_ref):
    spots = lax.broadcasted_iota(jnp.int32, (GROUP, GROUP), 0)
    chosen = (slot_ref[...] == spots).astype(FULL).astype(HALF)
    topic = topic_ref[...]
    out_ref[...] = exact_select(chosen, topic)
    column = jnp.sum(topic * mix_ref[...].astype(FULL), axis=0, keepdims=True)
    column_ref[...] = jnp.broadcast_to(column, column_ref.shape)


def pack_topics(slots, topic_sum, mix):
    return pl.pallas_call(
        pack_kernel,
        out_shape=[
            jax.ShapeDtypeStruct((GROUP, TOPICS), FULL),
            jax.ShapeDtypeStruct((TUP, TOPICS), FULL),
        ],
        compiler_params=pltpu.CompilerParams(vmem_limit_bytes=24 * 2**20),
        name="pack_topics",
    )(slots.reshape(1, GROUP), topic_sum, mix)


def place_kernel(ask_ref, came_ref, out_ref):
    spots = lax.broadcasted_iota(jnp.int32, (ROWS, GROUP), 0)
    chosen = (ask_ref[...] == spots).astype(FULL).astype(HALF)
    out_ref[...] = exact_select(chosen, came_ref[...])


def place_topics(asked, came):
    return pl.pallas_call(
        place_kernel,
        out_shape=jax.ShapeDtypeStruct((ROWS, TOPICS), FULL),
        compiler_params=pltpu.CompilerParams(vmem_limit_bytes=24 * 2**20),
        name="place_topics",
    )(asked.reshape(1, GROUP), came)


def trade(values, axis):
    return lax.all_to_all(values, axis, split_axis=0, concat_axis=0, tiled=True)


def shift_y(values, s):
    return lax.ppermute(values, "y", [(i, (i + s) % YS) for i in range(YS)])


def on_device(counts, lengths, tuple_map, topic_mix, word_probs):
    here = lax.axis_index("y").astype(jnp.int32).reshape(1)
    word_local = word_probs[0]
    gathered, at = [], 0
    for width in CHUNKS:
        gathered.append(lax.all_gather(word_local[at : at + width], "z", axis=0, tiled=False))
        at += width

    ids = tuple_map[0]
    owner = ids // ROWS
    order = jnp.arange(ROWS, dtype=jnp.int32)
    earlier = (owner[:, None] == owner[None, :]) & (order[None, :] < order[:, None])
    rank = jnp.sum(earlier.astype(jnp.int32), axis=1)
    key = owner * EACH + rank
    hit = key[None, :] == order[:, None]
    wanted = jnp.sum(jnp.where(hit, (ids % ROWS)[None, :], 0), axis=1)
    came_ids = trade(wanted.reshape(TUP, 1, EACH), ("z", "y")).reshape(ZS, YS, EACH)
    slot = owner * (YS * EACH) + rank
    slots = jnp.stack([slot if s == 0 else shift_y(slot, s) + s * EACH for s in range(YS)])

    sent = split_counts(counts[0], lengths[0].reshape(ROWS, 1), here)
    parts = []
    for c in range(len(CHUNKS)):
        parts.append(
            [sent[c * YS]] + [shift_y(sent[c * YS + s], s) for s in range(1, YS)]
        )

    asked = jnp.stack([jnp.roll(came_ids, s, axis=1) for s in range(YS)], axis=2).reshape(GROUP)
    given = give_mix(asked, topic_mix)
    arrived = trade(given.reshape(TUP, YS * EACH, TOPICS), ("z", "y")).reshape(GROUP, TOPICS)
    mix, turned = fetch_mix(slots, arrived)

    topic_sum = jnp.zeros((GROUP, TOPICS), FULL)
    word_sums = []
    for c, width in enumerate(CHUNKS):
        topic_sum, word_sum = ratio_pass(parts[c], mix, turned, gathered[c], topic_sum, width)
        word_sums.append(lax.psum_scatter(word_sum, "z", scatter_dimension=0, tiled=True)[0])

    packed, column = pack_topics(slots, topic_sum, mix)
    came = trade(packed.reshape(TUP, YS * EACH, TOPICS), ("z", "y")).reshape(GROUP, TOPICS)
    columns = trade(column.reshape(TUP, 1, TOPICS), ("z", "y"))
    placed = place_topics(asked, came)
    share = ROWS // LANG
    totals = jnp.sum(trade(placed.reshape(LANG, share, TOPICS), ("x", "core")), axis=0)
    own = lax.axis_index("x") * CS + lax.axis_index("core")
    mix_own = lax.dynamic_slice_in_dim(topic_mix, own * share, share, 0).astype(FULL)
    mixed = mix_own * totals
    update = TOPICS * mixed / jnp.sum(mixed, 1, keepdims=True)
    mix_update = trade(
        jnp.broadcast_to(update[None], (LANG, share, TOPICS)), ("x", "core")
    ).reshape(ROWS, TOPICS)

    total = jnp.sum(columns, axis=(0, 1))
    word_sum = jnp.concatenate([w.T for w in word_sums], axis=0)
    scaled = word_local.astype(FULL) * word_sum
    word_update = (VOCAB * scaled / total[None, :])[None]
    return (mix_update, word_update)


def solution(mesh):
    grid = Mesh(mesh.devices.reshape(ZS, YS, XS, CS), ("z", "y", "x", "core"))
    tup, lang = ("z", "y"), ("x", "core")
    return jax.shard_map(
        on_device,
        mesh=grid,
        in_specs=(P(lang, tup, None), P(lang, tup), P(lang, tup), P(tup, None), P(lang, tup, None)),
        out_specs=(P(tup, None), P(lang, tup, None)),
        check_vma=False,
    )
```

```python
import functools

import jax
import jax.numpy as jnp
import numpy as np
from jax import lax
from jax.experimental import pallas as pl
from jax.experimental.pallas import tpu as pltpu
from jax.sharding import Mesh
from jax.sharding import PartitionSpec as P

ZS, YS, XS, CS = 8, 4, 4, 2
TUP = ZS * YS
LANG = XS * CS
ROWS = 128
TOPICS = 256
SHARD = 512
VOCAB = 16384
LANES = 128
GROUP = YS * ROWS
EACH = ROWS // TUP
PART = YS * EACH
SPLIT = 2
CHUNKS = (384, 128)
HALF = jnp.bfloat16
FULL = jnp.float32
SHORT = jnp.float16
VMEM = 60 * 2**20


def iota(shape, dim):
    return lax.broadcasted_iota(jnp.int32, shape, dim)


def ones_where(mask):
    return mask.astype(FULL).astype(HALF)


def to_column(row):
    square = (row.shape[1], row.shape[1])
    return jnp.sum(jnp.where(iota(square, 0) == iota(square, 1), row, 0), axis=1, keepdims=True)


def to_row(column):
    square = (column.shape[0], column.shape[0])
    return jnp.sum(jnp.where(iota(square, 0) == iota(square, 1), column, 0), axis=0, keepdims=True)


def note_kernel(y_ref, id_ref, most_ref, step_ref, word_ref, note_ref, want_ref, word_out):
    square = (ROWS, ROWS)
    ids = id_ref[...]
    owner = ids // ROWS
    owner_column = to_column(owner)
    same = owner_column == owner
    rank = jnp.sum((same & (iota(square, 0) < iota(square, 1))).astype(jnp.int32), axis=0, keepdims=True)
    rank_column = jnp.sum((same & (iota(square, 1) < iota(square, 0))).astype(jnp.int32), axis=1, keepdims=True)
    note_ref[...] = owner * PART + y_ref[0] * EACH + rank
    local = to_column(ids % ROWS).astype(FULL)
    spread = jnp.where(rank_column == iota(square, 1), local, 0.0).astype(HALF)
    mine = ones_where(owner == iota((TUP, ROWS), 0))
    wanted = jnp.dot(mine, spread, preferred_element_type=FULL).astype(jnp.int32)
    most = jnp.max(jnp.max(most_ref[...], axis=0, keepdims=True), axis=1, keepdims=True)
    level = jnp.sum((most > step_ref[...]).astype(jnp.int32), axis=1, keepdims=True)
    want_ref[...] = jnp.where(iota((TUP, ROWS), 1) == EACH, level, wanted)[:, : EACH + 1]
    word_out[...] = word_ref[...]


def split_kernel(y_ref, len_ref, count_ref, most_ref, *out_refs):
    block = pl.program_id(0)
    here = y_ref[0]
    spans = to_column(len_ref[...])
    per = SHARD // LANES
    most = None
    for b in range(SPLIT):
        for s in range(YS):
            there = lax.rem(here + s, YS)
            q = 0
            for c, width in enumerate(CHUNKS):
                for p in range(width // LANES):
                    tile = ((block * SPLIT + b) * YS + there) * per + q
                    begin = pl.multiple_of((b * YS + there) * SHARD + q * LANES, LANES)
                    part = count_ref[:, pl.ds(begin, LANES)]
                    at = b * width + p * LANES
                    live = part * ones_where(tile < spans)
                    out_refs[c * YS + s][:, at : at + LANES] = live
                    most = live if most is None else jnp.maximum(most, live)
                    q += 1
    most = most.astype(FULL)

    @pl.when(block == 0)
    def _():
        most_ref[...] = most

    @pl.when(block > 0)
    def _():
        most_ref[...] = jnp.maximum(most_ref[...], most)


def split_counts(count_rows, lengths, here):
    steps = ZS // SPLIT
    return pl.pallas_call(
        split_kernel,
        grid_spec=pltpu.PrefetchScalarGridSpec(
            num_scalar_prefetch=1,
            grid=(steps,),
            in_specs=[
                pl.BlockSpec((1, ROWS), lambda i, y: (0, 0)),
                pl.BlockSpec((ROWS, SPLIT * YS * SHARD), lambda i, y: (0, i)),
            ],
            out_specs=[pl.BlockSpec((ROWS, LANES), lambda i, y: (0, 0))]
            + [pl.BlockSpec((ROWS, SPLIT * w), lambda i, y: (0, i)) for w in CHUNKS for _ in range(YS)],
        ),
        out_shape=[jax.ShapeDtypeStruct((ROWS, LANES), FULL)]
        + [jax.ShapeDtypeStruct((ROWS, ZS * w), HALF) for w in CHUNKS for _ in range(YS)],
        compiler_params=pltpu.CompilerParams(vmem_limit_bytes=VMEM),
        cost_estimate=pl.CostEstimate(flops=2**21, bytes_accessed=2**23, transcendentals=0),
        name="split_counts",
    )(here, lengths, count_rows)


def call(kernel, shapes, name, *args, scalars=0, after=(), passes=0):
    count = len(args)

    def body(*refs):
        kernel(*refs[:count], *refs[count + len(after) :])

    return pl.pallas_call(
        body,
        in_specs=[pl.BlockSpec(memory_space=pltpu.SMEM)] * scalars
        + [pl.BlockSpec(memory_space=pltpu.VMEM)] * (count - scalars)
        + [pl.BlockSpec(memory_space=pl.ANY)] * len(after),
        out_specs=jax.tree.map(lambda _: pl.BlockSpec(memory_space=pltpu.VMEM), shapes),
        out_shape=shapes,
        compiler_params=pltpu.CompilerParams(vmem_limit_bytes=16 * 2**20),
        cost_estimate=pl.CostEstimate(
            flops=2 * passes * GROUP * GROUP * TOPICS, bytes_accessed=2**18, transcendentals=0
        ),
        name=name,
    )(*args, *after)


def asked_column(came_ref):
    each = ones_where(iota((ROWS, TUP), 0) // EACH == iota((ROWS, TUP), 1))
    wide = jnp.dot(each, came_ref[:, :EACH].astype(FULL).astype(HALF), preferred_element_type=FULL)
    shape = (ROWS, EACH)
    picked = jnp.where(iota(shape, 0) % EACH == iota(shape, 1), wide, 0.0)
    return jnp.sum(picked, axis=1, keepdims=True).astype(jnp.int32)


def give_kernel(came_ref, topic_ref, out_ref):
    chosen = ones_where(asked_column(came_ref) == iota((ROWS, ROWS), 1))
    rows = jnp.dot(chosen, topic_ref[...], preferred_element_type=FULL).astype(HALF)
    for z in range(ZS):
        for y in range(YS):
            out_ref[z, y] = rows[z * PART : (z + 1) * PART]


def places(slot, here):
    owner = slot // PART
    behind = (here + YS - owner % YS) % YS
    return behind * ROWS + owner // YS * PART + slot % PART


def fetch_kernel(*refs):
    note_refs = refs[:YS]
    came_ref, scale_ref, arrived_ref, mix_ref, turned_ref, total_scale_ref = refs[YS:]
    level = jnp.max(came_ref[:, EACH:].astype(FULL), axis=0, keepdims=True)
    hit = iota((1, LANES), 1).astype(FULL) == level
    scale = jnp.sum(jnp.where(hit, scale_ref[...], 0.0), axis=1, keepdims=True)
    total_scale_ref[...] = jnp.broadcast_to(scale, total_scale_ref.shape)
    arrived = arrived_ref[...]
    for s in range(YS):
        chosen = ones_where(to_column(note_refs[s][...]) == iota((ROWS, GROUP), 1))
        mix = jnp.dot(chosen, arrived, preferred_element_type=FULL)
        mix_ref[s * ROWS : (s + 1) * ROWS, :] = mix.astype(HALF)
        turned_ref[:, s * ROWS : (s + 1) * ROWS] = (mix.T * scale).astype(HALF)


def pack(here, note_refs, topic, mix, out_refs):
    column = jnp.sum(topic * mix.astype(FULL), axis=0, keepdims=True)
    chosen = jnp.concatenate(
        [ones_where(places(r[...], here) == iota((GROUP, ROWS), 0)) for r in note_refs], axis=1
    )
    packed = exact_select(chosen, topic)
    for s in range(YS):
        out_refs[s][:ROWS, :] = packed[s * ROWS : (s + 1) * ROWS, :]
        out_refs[s][ROWS:, :] = jnp.broadcast_to(column, (8, TOPICS))


def join_kernel(*refs):
    out_ref, zero_ref = refs[YS:]
    zero_ref[...] = jnp.zeros_like(zero_ref)
    for z in range(ZS):
        rows = slice(z * PART, (z + 1) * PART)
        out_ref[z, :PART, :] = sum(r[rows, :] for r in refs[:YS])
        out_ref[z, PART:, :] = sum(r[ROWS:, :] for r in refs[:YS])


def place_kernel(came_ref, topic_ref, scale_ref, out_ref, total_ref, zero_ref):
    zero_ref[...] = jnp.zeros_like(zero_ref)
    asked = to_row(asked_column(came_ref))
    chosen = ones_where(asked == iota((ROWS, ROWS), 0))
    rows = topic_ref[:, :PART, :].reshape(ROWS, TOPICS)
    out_ref[...] = exact_select(chosen, rows)
    total_ref[...] = jnp.sum(topic_ref[:, PART:, :], axis=0) * scale_ref[0:1, 0:1]


def exact_select(chosen, values):
    total = None
    rest = values
    for _ in range(3):
        piece = rest.astype(HALF)
        rest = rest - piece.astype(FULL)
        term = jnp.dot(chosen, piece, preferred_element_type=FULL)
        total = term if total is None else total + term
    return total


def trade(values, axis):
    return lax.all_to_all(values, axis, split_axis=0, concat_axis=0, tiled=True)


def shift_y(values, s):
    return lax.ppermute(values, "y", [(i, (i + s) % YS) for i in range(YS)])


def shift_z(values, s):
    return lax.ppermute(values, "z", [(i, (i + s) % ZS) for i in range(ZS)])


def ring_gather(block):
    found = {0: block}
    up = down = block
    for t in range(1, ZS // 2 + 1):
        up = found[ZS - t] = shift_z(up, 1)
        if t < ZS // 2:
            down = found[t] = shift_z(down, ZS - 1)
    return found


NEAR = (4, 5, 3, 6, 2, 7, 1, 0)
def ratio_kernel(order_ref, y_ref, *refs):
    count_refs, refs = refs[: YS * len(CHUNKS)], refs[YS * len(CHUNKS) :]
    note_refs, refs = refs[:YS], refs[YS:]
    given_refs, refs = refs[:ZS], refs[ZS:]
    mix_ref, turned_ref, refs = refs[0], refs[1], refs[2:]
    pack_refs, refs = refs[:YS], refs[YS:]
    up_ref, down_ref, rest_ref, topic_ref, word_ref, sum_ref = refs
    step = pl.program_id(0)
    for i, ref in enumerate(given_refs):

        @pl.when(step == i)
        def _(ref=ref):
            word_ref[...] = ref[...]

    mix, turned = mix_ref[...], turned_ref[...]
    words = word_ref[...]
    counts = jnp.concatenate(
        [
            jnp.concatenate([r[...] for r in count_refs[c * YS : (c + 1) * YS]], axis=0)
            for c in range(len(CHUNKS))
        ],
        axis=1,
    )
    expected = lax.dot_general(
        mix, words, (((1,), (1,)), ((), ())), preferred_element_type=FULL
    )
    ratios = counts.astype(FULL) * pl.reciprocal(expected)
    high = ratios.astype(HALF)
    low = (ratios - high.astype(FULL)).astype(HALF)
    topic = jnp.dot(
        jnp.concatenate([high, low], axis=1),
        jnp.concatenate([words, words], axis=0),
        preferred_element_type=FULL,
    )
    sum_ref[...] = jnp.dot(
        jnp.concatenate([turned, turned], axis=1),
        jnp.concatenate([high, low], axis=0),
        preferred_element_type=FULL,
    )

    @pl.when(step == 0)
    def _():
        topic_ref[...] = topic
        up_ref[...] = sum_ref[...]

    @pl.when(step > 0)
    def _():
        topic_ref[...] += topic

    @pl.when(step == 1)
    def _():
        down_ref[...] = sum_ref[...]

    @pl.when(step > 1)
    def _():
        rest_ref[0] = sum_ref[...]

    @pl.when(step == ZS - 1)
    def _():
        pack(y_ref[0], note_refs, topic_ref[...], mix, pack_refs)


def ratio_pass(parts, notes, words, mix, turned, order, here):
    def whole(*shape):
        return pl.BlockSpec(shape, lambda i, o, y: (0,) * len(shape))

    block = (TOPICS, SHARD)
    return pl.pallas_call(
        ratio_kernel,
        grid_spec=pltpu.PrefetchScalarGridSpec(
            num_scalar_prefetch=2,
            grid=(ZS,),
            in_specs=[pl.BlockSpec((ROWS, w), lambda i, o, y: (0, o[i])) for w in CHUNKS for _ in range(YS)]
            + [whole(1, ROWS)] * YS
            + [whole(SHARD, TOPICS)] * ZS
            + [whole(GROUP, TOPICS), whole(TOPICS, GROUP)],
            out_specs=[whole(ROWS + 8, TOPICS)] * YS
            + [
                whole(*block),
                whole(*block),
                pl.BlockSpec((1, *block), lambda i, o, y: (jnp.maximum(i - 2, 0), 0, 0)),
            ],
            scratch_shapes=[
                pltpu.VMEM((GROUP, TOPICS), FULL),
                pltpu.VMEM((SHARD, TOPICS), HALF),
                pltpu.VMEM(block, FULL),
            ],
        ),
        out_shape=[jax.ShapeDtypeStruct((ROWS + 8, TOPICS), FULL)] * YS
        + [
            jax.ShapeDtypeStruct(block, FULL),
            jax.ShapeDtypeStruct(block, FULL),
            jax.ShapeDtypeStruct((ZS - 2, *block), FULL),
        ],
        compiler_params=pltpu.CompilerParams(vmem_limit_bytes=VMEM),
        cost_estimate=pl.CostEstimate(
            flops=10 * GROUP * ZS * SHARD * TOPICS,
            bytes_accessed=ZS * SHARD * (2 * GROUP + 6 * TOPICS),
            transcendentals=GROUP * ZS * SHARD,
        ),
        name="ratio_pass",
    )(order, here, *parts, *notes, *words, mix, turned)


PLACE = {near: i for i, near in enumerate(NEAR[2:])}
STRIP = 256


def ring_add(came, rest, near, zero):
    return (came.astype(FULL) + (rest[PLACE[near]] + zero[0, 0])).astype(SHORT)


def last_kernel(sum_ref, word_ref, total_ref, out_ref):
    out_ref[0] = word_ref[...].astype(FULL) * sum_ref[...].T * (VOCAB / total_ref[0:1, :])


def last_step(sums, words, total):
    return pl.pallas_call(
        last_kernel,
        grid=(SHARD // STRIP,),
        in_specs=[
            pl.BlockSpec((TOPICS, STRIP), lambda i: (0, i)),
            pl.BlockSpec((STRIP, TOPICS), lambda i: (i, 0)),
            pl.BlockSpec((8, TOPICS), lambda i: (0, 0)),
        ],
        out_specs=pl.BlockSpec((1, STRIP, TOPICS), lambda i: (0, i, 0)),
        out_shape=jax.ShapeDtypeStruct((1, SHARD, TOPICS), FULL),
        compiler_params=pltpu.CompilerParams(vmem_limit_bytes=16 * 2**20),
        cost_estimate=pl.CostEstimate(flops=2**18, bytes_accessed=2**20, transcendentals=0),
        name="word_update",
    )(sums, words, total)


def on_device(counts, lengths, tuple_map, topic_mix, word_probs):
    here = lax.axis_index("y").astype(jnp.int32).reshape(1)
    order = (lax.axis_index("z") + jnp.array(NEAR, jnp.int32)) % ZS
    steps = jnp.asarray(np.ldexp(1.0, np.arange(LANES) - 120), FULL).reshape(1, LANES)
    scales = jnp.asarray(np.ldexp(1.0, 122 - np.arange(LANES)), FULL).reshape(1, LANES)
    most, *sent = split_counts(counts[0], lengths, here)
    parts = [
        [sent[c * YS]] + [shift_y(sent[c * YS + s], s) for s in range(1, YS)]
        for c in range(len(CHUNKS))
    ]
    note, wanted, word_local = call(
        note_kernel,
        [
            jax.ShapeDtypeStruct((1, ROWS), jnp.int32),
            jax.ShapeDtypeStruct((TUP, EACH + 1), jnp.int32),
            jax.ShapeDtypeStruct((SHARD, TOPICS), HALF),
        ],
        "note", here, tuple_map, most, steps, word_probs[0], scalars=1,
    )
    notes = [note] + [shift_y(note, s) for s in range(1, YS)]
    found = ring_gather(word_local)
    words = [found[n] for n in NEAR]
    came_ids = trade(wanted.reshape(TUP, 1, EACH + 1), ("z", "y")).reshape(TUP, EACH + 1)
    given = call(
        give_kernel, jax.ShapeDtypeStruct((ZS, YS, PART, TOPICS), HALF), "give",
        came_ids, topic_mix, after=parts[0][1:],
    )
    arrived = trade(given.reshape(TUP, PART, TOPICS), ("z", "y")).reshape(GROUP, TOPICS)
    mix, turned, scale = call(
        fetch_kernel,
        [
            jax.ShapeDtypeStruct((GROUP, TOPICS), HALF),
            jax.ShapeDtypeStruct((TOPICS, GROUP), HALF),
            jax.ShapeDtypeStruct((8, LANES), FULL),
        ],
        "fetch", *notes, came_ids, scales, arrived, after=parts[1][1:],
    )

    *packed, up, down, rest = ratio_pass(sum(parts, []), notes, words, mix, turned, order, here)
    back = [packed[0]] + [shift_y(packed[s], YS - s) for s in range(1, YS)]
    up, down = shift_z(up.astype(SHORT), 1), shift_z(down.astype(SHORT), ZS - 1)
    zero = jax.ShapeDtypeStruct((8, LANES), FULL)
    joined, zero_join = call(
        join_kernel, [jax.ShapeDtypeStruct((ZS, PART + 8, TOPICS), FULL), zero], "join", *back
    )
    came = trade(joined, "z")
    up, down = ring_add(up, rest, 3, zero_join), ring_add(down, rest, 6, zero_join)
    up, down = shift_z(up, 1), shift_z(down, ZS - 1)
    placed, total, zero_place = call(
        place_kernel,
        [jax.ShapeDtypeStruct((ROWS, TOPICS), FULL), jax.ShapeDtypeStruct((8, TOPICS), FULL), zero],
        "place", came_ids, came, scale,
    )
    share = ROWS // LANG
    shares = trade(placed.reshape(LANG, share, TOPICS), ("x", "core"))
    up, down = ring_add(up, rest, 2, zero_place), ring_add(down, rest, 7, zero_place)
    up, down = shift_z(up, 1), shift_z(down, ZS - 1)
    totals = jnp.sum(shares, axis=0)
    own = lax.axis_index("x") * CS + lax.axis_index("core")
    mix_own = lax.dynamic_slice_in_dim(topic_mix, own * share, share, 0).astype(FULL)
    mixed = mix_own * totals
    update = TOPICS * mixed / jnp.sum(mixed, 1, keepdims=True)
    mix_update = trade(
        jnp.broadcast_to(update[None], (LANG, share, TOPICS)), ("x", "core")
    ).reshape(ROWS, TOPICS)
    up = shift_z(ring_add(up, rest, 1, zero_place), 1)
    sums = up.astype(FULL) + down.astype(FULL) + rest[PLACE[0]]
    return (mix_update, last_step(sums, word_probs[0], total))


def solution(mesh):
    grid = Mesh(mesh.devices.reshape(ZS, YS, XS, CS), ("z", "y", "x", "core"))
    tup, lang = ("z", "y"), ("x", "core")
    return jax.shard_map(
        on_device,
        mesh=grid,
        in_specs=(P(lang, tup, None), P(lang, tup), P(lang, tup), P(tup, None), P(lang, tup, None)),
        out_specs=(P(tup, None), P(lang, tup, None)),
        check_vma=False,
    )
```

```python
import functools

import jax
import jax.numpy as jnp
import numpy as np
from jax import lax
from jax.experimental import pallas as pl
from jax.experimental.pallas import tpu as pltpu
from jax.sharding import Mesh
from jax.sharding import PartitionSpec as P

ZS, YS, XS, CS = 8, 4, 4, 2
TUP = ZS * YS
LANG = XS * CS
ROWS = 128
TOPICS = 256
SHARD = 512
VOCAB = 16384
LANES = 128
GROUP = YS * ROWS
EACH = ROWS // TUP
PART = YS * EACH
SPLIT = 2
CHUNKS = (384, 128)
HALF = jnp.bfloat16
FULL = jnp.float32
SHORT = jnp.float16
VMEM = 60 * 2**20


def iota(shape, dim):
    return lax.broadcasted_iota(jnp.int32, shape, dim)


def ones_where(mask):
    return mask.astype(FULL).astype(HALF)


def to_column(row):
    square = (row.shape[1], row.shape[1])
    return jnp.sum(jnp.where(iota(square, 0) == iota(square, 1), row, 0), axis=1, keepdims=True)


def to_row(column):
    square = (column.shape[0], column.shape[0])
    return jnp.sum(jnp.where(iota(square, 0) == iota(square, 1), column, 0), axis=0, keepdims=True)


def note_kernel(y_ref, id_ref, most_ref, step_ref, word_ref, note_ref, want_ref, word_out):
    square = (ROWS, ROWS)
    ids = id_ref[...]
    owner = ids // ROWS
    owner_column = to_column(owner)
    same = owner_column == owner
    rank = jnp.sum((same & (iota(square, 0) < iota(square, 1))).astype(jnp.int32), axis=0, keepdims=True)
    rank_column = jnp.sum((same & (iota(square, 1) < iota(square, 0))).astype(jnp.int32), axis=1, keepdims=True)
    note_ref[...] = owner * PART + y_ref[0] * EACH + rank
    local = to_column(ids % ROWS).astype(FULL)
    spread = jnp.where(rank_column == iota(square, 1), local, 0.0).astype(HALF)
    mine = ones_where(owner == iota((TUP, ROWS), 0))
    wanted = jnp.dot(mine, spread, preferred_element_type=FULL).astype(jnp.int32)
    most = jnp.max(jnp.max(most_ref[...], axis=0, keepdims=True), axis=1, keepdims=True)
    level = jnp.sum((most > step_ref[...]).astype(jnp.int32), axis=1, keepdims=True)
    want_ref[...] = jnp.where(iota((TUP, ROWS), 1) == EACH, level, wanted)[:, : EACH + 1]
    word_out[...] = word_ref[...]


def split_kernel(y_ref, len_ref, count_ref, most_ref, *out_refs):
    block = pl.program_id(0)
    here = y_ref[0]
    spans = to_column(len_ref[...])
    per = SHARD // LANES
    most = None
    for b in range(SPLIT):
        for s in range(YS):
            there = lax.rem(here + s, YS)
            q = 0
            for c, width in enumerate(CHUNKS):
                for p in range(width // LANES):
                    tile = ((block * SPLIT + b) * YS + there) * per + q
                    begin = pl.multiple_of((b * YS + there) * SHARD + q * LANES, LANES)
                    part = count_ref[:, pl.ds(begin, LANES)]
                    at = b * width + p * LANES
                    live = part * ones_where(tile < spans)
                    out_refs[c * YS + s][:, at : at + LANES] = live
                    most = live if most is None else jnp.maximum(most, live)
                    q += 1
    most = most.astype(FULL)

    @pl.when(block == 0)
    def _():
        most_ref[...] = most

    @pl.when(block > 0)
    def _():
        most_ref[...] = jnp.maximum(most_ref[...], most)


def split_counts(count_rows, lengths, here):
    steps = ZS // SPLIT
    return pl.pallas_call(
        split_kernel,
        grid_spec=pltpu.PrefetchScalarGridSpec(
            num_scalar_prefetch=1,
            grid=(steps,),
            in_specs=[
                pl.BlockSpec((1, ROWS), lambda i, y: (0, 0)),
                pl.BlockSpec((ROWS, SPLIT * YS * SHARD), lambda i, y: (0, i)),
            ],
            out_specs=[pl.BlockSpec((ROWS, LANES), lambda i, y: (0, 0))]
            + [pl.BlockSpec((ROWS, SPLIT * w), lambda i, y: (0, i)) for w in CHUNKS for _ in range(YS)],
        ),
        out_shape=[jax.ShapeDtypeStruct((ROWS, LANES), FULL)]
        + [jax.ShapeDtypeStruct((ROWS, ZS * w), HALF) for w in CHUNKS for _ in range(YS)],
        compiler_params=pltpu.CompilerParams(vmem_limit_bytes=VMEM),
        cost_estimate=pl.CostEstimate(flops=2**21, bytes_accessed=2**23, transcendentals=0),
        name="split_counts",
    )(here, lengths, count_rows)


def call(kernel, shapes, name, *args, scalars=0, after=(), passes=0):
    count = len(args)

    def body(*refs):
        kernel(*refs[:count], *refs[count + len(after) :])

    return pl.pallas_call(
        body,
        in_specs=[pl.BlockSpec(memory_space=pltpu.SMEM)] * scalars
        + [pl.BlockSpec(memory_space=pltpu.VMEM)] * (count - scalars)
        + [pl.BlockSpec(memory_space=pl.ANY)] * len(after),
        out_specs=jax.tree.map(lambda _: pl.BlockSpec(memory_space=pltpu.VMEM), shapes),
        out_shape=shapes,
        compiler_params=pltpu.CompilerParams(vmem_limit_bytes=16 * 2**20),
        cost_estimate=pl.CostEstimate(
            flops=2 * passes * GROUP * GROUP * TOPICS, bytes_accessed=2**18, transcendentals=0
        ),
        name=name,
    )(*args, *after)


def asked_column(came_ref):
    each = ones_where(iota((ROWS, TUP), 0) // EACH == iota((ROWS, TUP), 1))
    wide = jnp.dot(each, came_ref[:, :EACH].astype(FULL).astype(HALF), preferred_element_type=FULL)
    shape = (ROWS, EACH)
    picked = jnp.where(iota(shape, 0) % EACH == iota(shape, 1), wide, 0.0)
    return jnp.sum(picked, axis=1, keepdims=True).astype(jnp.int32)


def give_kernel(came_ref, topic_ref, out_ref):
    chosen = ones_where(asked_column(came_ref) == iota((ROWS, ROWS), 1))
    rows = jnp.dot(chosen, topic_ref[...], preferred_element_type=FULL).astype(HALF)
    for z in range(ZS):
        for y in range(YS):
            out_ref[z, y] = rows[z * PART : (z + 1) * PART]


def places(slot, here):
    owner = slot // PART
    behind = (here + YS - owner % YS) % YS
    return behind * ROWS + owner // YS * PART + slot % PART


def fetch_kernel(*refs):
    note_refs = refs[:YS]
    came_ref, scale_ref, arrived_ref, mix_ref, turned_ref, total_scale_ref = refs[YS:]
    level = jnp.max(came_ref[:, EACH:].astype(FULL), axis=0, keepdims=True)
    hit = iota((1, LANES), 1).astype(FULL) == level
    scale = jnp.sum(jnp.where(hit, scale_ref[...], 0.0), axis=1, keepdims=True)
    total_scale_ref[...] = jnp.broadcast_to(scale, total_scale_ref.shape)
    arrived = arrived_ref[...]
    for s in range(YS):
        chosen = ones_where(to_column(note_refs[s][...]) == iota((ROWS, GROUP), 1))
        mix = jnp.dot(chosen, arrived, preferred_element_type=FULL)
        mix_ref[s * ROWS : (s + 1) * ROWS, :] = mix.astype(HALF)
        turned_ref[:, s * ROWS : (s + 1) * ROWS] = (mix.T * scale).astype(HALF)


def pack(here, note_refs, topic, mix, out_refs):
    column = jnp.sum(topic * mix.astype(FULL), axis=0, keepdims=True)
    chosen = jnp.concatenate(
        [ones_where(places(r[...], here) == iota((GROUP, ROWS), 0)) for r in note_refs], axis=1
    )
    packed = exact_select(chosen, topic)
    for s in range(YS):
        out_refs[s][:ROWS, :] = packed[s * ROWS : (s + 1) * ROWS, :]
        out_refs[s][ROWS:, :] = jnp.broadcast_to(column, (8, TOPICS))


def join_kernel(*refs):
    out_ref = refs[YS]
    for z in range(ZS):
        rows = slice(z * PART, (z + 1) * PART)
        out_ref[z, :PART, :] = sum(r[rows, :] for r in refs[:YS])
        out_ref[z, PART:, :] = sum(r[ROWS:, :] for r in refs[:YS])


def place_kernel(came_ref, topic_ref, scale_ref, out_ref, total_ref):
    asked = to_row(asked_column(came_ref))
    chosen = ones_where(asked == iota((ROWS, ROWS), 0))
    rows = topic_ref[:, :PART, :].reshape(ROWS, TOPICS)
    out_ref[...] = exact_select(chosen, rows)
    total_ref[...] = jnp.sum(topic_ref[:, PART:, :], axis=0) * scale_ref[0:1, 0:1]


def exact_select(chosen, values):
    total = None
    rest = values
    for _ in range(3):
        piece = rest.astype(HALF)
        rest = rest - piece.astype(FULL)
        term = jnp.dot(chosen, piece, preferred_element_type=FULL)
        total = term if total is None else total + term
    return total


def trade(values, axis):
    return lax.all_to_all(values, axis, split_axis=0, concat_axis=0, tiled=True)


def shift_y(values, s):
    return lax.ppermute(values, "y", [(i, (i + s) % YS) for i in range(YS)])


def shift_z(values, s):
    return lax.ppermute(values, "z", [(i, (i + s) % ZS) for i in range(ZS)])


def ring_gather(block):
    found = {0: block}
    up = down = block
    for t in range(1, ZS // 2 + 1):
        up = found[ZS - t] = shift_z(up, 1)
        if t < ZS // 2:
            down = found[t] = shift_z(down, ZS - 1)
    return found


NEAR = (4, 5, 3, 6, 2, 7, 1, 0)
def ratio_kernel(order_ref, y_ref, *refs):
    count_refs, refs = refs[: YS * len(CHUNKS)], refs[YS * len(CHUNKS) :]
    note_refs, refs = refs[:YS], refs[YS:]
    given_refs, refs = refs[:ZS], refs[ZS:]
    mix_ref, turned_ref, refs = refs[0], refs[1], refs[2:]
    pack_refs, refs = refs[:YS], refs[YS:]
    up_ref, down_ref, rest_ref, topic_ref, word_ref, sum_ref = refs
    step = pl.program_id(0)
    for i, ref in enumerate(given_refs):

        @pl.when(step == i)
        def _(ref=ref):
            word_ref[...] = ref[...]

    mix, turned = mix_ref[...], turned_ref[...]
    words = word_ref[...]
    counts = jnp.concatenate(
        [
            jnp.concatenate([r[...] for r in count_refs[c * YS : (c + 1) * YS]], axis=0)
            for c in range(len(CHUNKS))
        ],
        axis=1,
    )
    expected = lax.dot_general(
        mix, words, (((1,), (1,)), ((), ())), preferred_element_type=FULL
    )
    ratios = counts.astype(FULL) * pl.reciprocal(expected)
    high = ratios.astype(HALF)
    low = (ratios - high.astype(FULL)).astype(HALF)
    topic = jnp.dot(
        jnp.concatenate([high, low], axis=1),
        jnp.concatenate([words, words], axis=0),
        preferred_element_type=FULL,
    )
    sum_ref[...] = jnp.dot(
        jnp.concatenate([turned, turned], axis=1),
        jnp.concatenate([high, low], axis=0),
        preferred_element_type=FULL,
    )

    @pl.when(step == 0)
    def _():
        topic_ref[...] = topic
        up_ref[...] = sum_ref[...]

    @pl.when(step > 0)
    def _():
        topic_ref[...] += topic

    @pl.when(step == 1)
    def _():
        down_ref[...] = sum_ref[...]

    @pl.when(step > 1)
    def _():
        rest_ref[0] = sum_ref[...]

    @pl.when(step == ZS - 1)
    def _():
        pack(y_ref[0], note_refs, topic_ref[...], mix, pack_refs)


def ratio_pass(parts, notes, words, mix, turned, order, here):
    def whole(*shape):
        return pl.BlockSpec(shape, lambda i, o, y: (0,) * len(shape))

    block = (TOPICS, SHARD)
    return pl.pallas_call(
        ratio_kernel,
        grid_spec=pltpu.PrefetchScalarGridSpec(
            num_scalar_prefetch=2,
            grid=(ZS,),
            in_specs=[pl.BlockSpec((ROWS, w), lambda i, o, y: (0, o[i])) for w in CHUNKS for _ in range(YS)]
            + [whole(1, ROWS)] * YS
            + [whole(SHARD, TOPICS)] * ZS
            + [whole(GROUP, TOPICS), whole(TOPICS, GROUP)],
            out_specs=[whole(ROWS + 8, TOPICS)] * YS
            + [
                whole(*block),
                whole(*block),
                pl.BlockSpec((1, *block), lambda i, o, y: (jnp.maximum(i - 2, 0), 0, 0)),
            ],
            scratch_shapes=[
                pltpu.VMEM((GROUP, TOPICS), FULL),
                pltpu.VMEM((SHARD, TOPICS), HALF),
                pltpu.VMEM(block, FULL),
            ],
        ),
        out_shape=[jax.ShapeDtypeStruct((ROWS + 8, TOPICS), FULL)] * YS
        + [
            jax.ShapeDtypeStruct(block, FULL),
            jax.ShapeDtypeStruct(block, FULL),
            jax.ShapeDtypeStruct((ZS - 2, *block), FULL),
        ],
        compiler_params=pltpu.CompilerParams(vmem_limit_bytes=VMEM),
        cost_estimate=pl.CostEstimate(
            flops=10 * GROUP * ZS * SHARD * TOPICS,
            bytes_accessed=ZS * SHARD * (2 * GROUP + 6 * TOPICS),
            transcendentals=GROUP * ZS * SHARD,
        ),
        name="ratio_pass",
    )(order, here, *parts, *notes, *words, mix, turned)


PLACE = {near: i for i, near in enumerate(NEAR[2:])}
STRIP = 256


def ring_add(came, rest, near, zero=0.0):
    return (came.astype(FULL) + (rest[PLACE[near]] + zero)).astype(SHORT)


def zero_of(arrays):
    least = 0.0
    for a in arrays:
        least = jnp.minimum(least, jnp.abs(a[0, 0]))
    return least


def sample(*arrays):
    return sum(a[:8, :LANES].astype(FULL) for a in arrays)


def share_kernel(own_ref, part_ref, mix_ref, out_ref):
    share = ROWS // LANG
    begin = pl.multiple_of(own_ref[0] * share, share)
    mixed = mix_ref[pl.ds(begin, share), :].astype(FULL) * jnp.sum(part_ref[...], axis=0)
    update = TOPICS * mixed / jnp.sum(mixed, axis=1, keepdims=True)
    out_ref[...] = jnp.broadcast_to(update[None], out_ref.shape)


def last_kernel(sum_ref, word_ref, total_ref, out_ref):
    out_ref[0] = word_ref[...].astype(FULL) * sum_ref[...].T * (VOCAB / total_ref[0:1, :])


def last_step(sums, words, total):
    return pl.pallas_call(
        last_kernel,
        grid=(SHARD // STRIP,),
        in_specs=[
            pl.BlockSpec((TOPICS, STRIP), lambda i: (0, i)),
            pl.BlockSpec((STRIP, TOPICS), lambda i: (i, 0)),
            pl.BlockSpec((8, TOPICS), lambda i: (0, 0)),
        ],
        out_specs=pl.BlockSpec((1, STRIP, TOPICS), lambda i: (0, i, 0)),
        out_shape=jax.ShapeDtypeStruct((1, SHARD, TOPICS), FULL),
        compiler_params=pltpu.CompilerParams(vmem_limit_bytes=16 * 2**20),
        cost_estimate=pl.CostEstimate(flops=2**18, bytes_accessed=2**20, transcendentals=0),
        name="word_update",
    )(sums, words, total)


def on_device(counts, lengths, tuple_map, topic_mix, word_probs):
    here = lax.axis_index("y").astype(jnp.int32).reshape(1)
    order = (lax.axis_index("z") + jnp.array(NEAR, jnp.int32)) % ZS
    steps = jnp.asarray(np.ldexp(1.0, np.arange(LANES) - 120), FULL).reshape(1, LANES)
    scales = jnp.asarray(np.ldexp(1.0, 122 - np.arange(LANES)), FULL).reshape(1, LANES)
    most, *sent = split_counts(counts[0], lengths, here)
    parts = [
        [sent[c * YS]] + [shift_y(sent[c * YS + s], s) for s in range(1, YS)]
        for c in range(len(CHUNKS))
    ]
    note, wanted, word_local = call(
        note_kernel,
        [
            jax.ShapeDtypeStruct((1, ROWS), jnp.int32),
            jax.ShapeDtypeStruct((TUP, EACH + 1), jnp.int32),
            jax.ShapeDtypeStruct((SHARD, TOPICS), HALF),
        ],
        "note", here, tuple_map, most, steps, word_probs[0], scalars=1,
    )
    notes = [note] + [shift_y(note, s) for s in range(1, YS)]
    found = ring_gather(word_local)
    words = [found[n] for n in NEAR]
    came_ids = trade(wanted.reshape(TUP, 1, EACH + 1), ("z", "y")).reshape(TUP, EACH + 1)
    given = call(
        give_kernel, jax.ShapeDtypeStruct((ZS, YS, PART, TOPICS), HALF), "give",
        came_ids, topic_mix, after=parts[0][1:],
    )
    arrived = trade(given.reshape(TUP, PART, TOPICS), ("z", "y")).reshape(GROUP, TOPICS)
    mix, turned, scale = call(
        fetch_kernel,
        [
            jax.ShapeDtypeStruct((GROUP, TOPICS), HALF),
            jax.ShapeDtypeStruct((TOPICS, GROUP), HALF),
            jax.ShapeDtypeStruct((8, LANES), FULL),
        ],
        "fetch", *notes, came_ids, scales, arrived, after=parts[1][1:],
    )

    *packed, up, down, rest = ratio_pass(sum(parts, []), notes, words, mix, turned, order, here)
    back = [packed[0]] + [shift_y(packed[s], YS - s) for s in range(1, YS)]
    up, down = shift_z(up.astype(SHORT), 1), shift_z(down.astype(SHORT), ZS - 1)
    zero = zero_of(back[1:])
    up, down = ring_add(up, rest, 3, zero), ring_add(down, rest, 6, zero)
    joined = call(
        join_kernel, jax.ShapeDtypeStruct((ZS, PART + 8, TOPICS), FULL), "join", *back, after=[sample(up)]
    )
    came = trade(joined, "z")
    up, down = shift_z(up, 1), shift_z(down, ZS - 1)
    up, down = ring_add(up, rest, 2), ring_add(down, rest, 7)
    placed, total = call(
        place_kernel,
        [jax.ShapeDtypeStruct((ROWS, TOPICS), FULL), jax.ShapeDtypeStruct((8, TOPICS), FULL)],
        "place", came_ids, came, scale, after=[sample(up)],
    )
    share = ROWS // LANG
    shares = trade(placed.reshape(LANG, share, TOPICS), ("x", "core"))
    up, down = shift_z(up, 1), shift_z(down, ZS - 1)
    up = ring_add(up, rest, 1)
    own = (lax.axis_index("x") * CS + lax.axis_index("core")).astype(jnp.int32).reshape(1)
    update = call(
        share_kernel, jax.ShapeDtypeStruct((LANG, share, TOPICS), FULL), "share",
        own, shares, topic_mix, scalars=1, after=[sample(up)],
    )
    mix_update = trade(update, ("x", "core")).reshape(ROWS, TOPICS)
    up = shift_z(up, 1)
    sums = up.astype(FULL) + down.astype(FULL) + rest[PLACE[0]]
    return (mix_update, last_step(sums, word_probs[0], total))


def solution(mesh):
    grid = Mesh(mesh.devices.reshape(ZS, YS, XS, CS), ("z", "y", "x", "core"))
    tup, lang = ("z", "y"), ("x", "core")
    return jax.shard_map(
        on_device,
        mesh=grid,
        in_specs=(P(lang, tup, None), P(lang, tup), P(lang, tup), P(tup, None), P(lang, tup, None)),
        out_specs=(P(tup, None), P(lang, tup, None)),
        check_vma=False,
    )
```

```python
import functools

import jax
import jax.numpy as jnp
import numpy as np
from jax import lax
from jax.experimental import pallas as pl
from jax.experimental.pallas import tpu as pltpu
from jax.sharding import Mesh
from jax.sharding import PartitionSpec as P

ZS, YS, XS, CS = 8, 4, 4, 2
TUP = ZS * YS
LANG = XS * CS
ROWS = 128
TOPICS = 256
SHARD = 512
VOCAB = 16384
LANES = 128
GROUP = YS * ROWS
EACH = ROWS // TUP
PART = YS * EACH
SPLIT = 2
CHUNKS = (384, 128)
HALF = jnp.bfloat16
FULL = jnp.float32
SHORT = jnp.float16
VMEM = 60 * 2**20


def iota(shape, dim):
    return lax.broadcasted_iota(jnp.int32, shape, dim)


def ones_where(mask):
    return mask.astype(FULL).astype(HALF)


def to_column(row):
    square = (row.shape[1], row.shape[1])
    return jnp.sum(jnp.where(iota(square, 0) == iota(square, 1), row, 0), axis=1, keepdims=True)


def to_row(column):
    square = (column.shape[0], column.shape[0])
    return jnp.sum(jnp.where(iota(square, 0) == iota(square, 1), column, 0), axis=0, keepdims=True)


def note_kernel(y_ref, id_ref, most_ref, step_ref, word_ref, note_ref, want_ref, word_out):
    square = (ROWS, ROWS)
    ids = id_ref[...]
    owner = ids // ROWS
    owner_column = to_column(owner)
    same = owner_column == owner
    rank = jnp.sum((same & (iota(square, 0) < iota(square, 1))).astype(jnp.int32), axis=0, keepdims=True)
    rank_column = jnp.sum((same & (iota(square, 1) < iota(square, 0))).astype(jnp.int32), axis=1, keepdims=True)
    note_ref[...] = owner * PART + y_ref[0] * EACH + rank
    local = to_column(ids % ROWS).astype(FULL)
    spread = jnp.where(rank_column == iota(square, 1), local, 0.0).astype(HALF)
    mine = ones_where(owner == iota((TUP, ROWS), 0))
    wanted = jnp.dot(mine, spread, preferred_element_type=FULL).astype(jnp.int32)
    most = jnp.max(jnp.max(most_ref[...], axis=0, keepdims=True), axis=1, keepdims=True)
    level = jnp.sum((most > step_ref[...]).astype(jnp.int32), axis=1, keepdims=True)
    want_ref[...] = jnp.where(iota((TUP, ROWS), 1) == EACH, level, wanted)[:, : EACH + 1]
    word_out[...] = word_ref[...]


def split_kernel(y_ref, len_ref, count_ref, most_ref, *out_refs):
    block = pl.program_id(0)
    here = y_ref[0]
    spans = to_column(len_ref[...])
    per = SHARD // LANES
    most = None
    for b in range(SPLIT):
        for s in range(YS):
            there = lax.rem(here + s, YS)
            q = 0
            for c, width in enumerate(CHUNKS):
                for p in range(width // LANES):
                    tile = ((block * SPLIT + b) * YS + there) * per + q
                    begin = pl.multiple_of((b * YS + there) * SHARD + q * LANES, LANES)
                    part = count_ref[:, pl.ds(begin, LANES)]
                    at = b * width + p * LANES
                    live = part * ones_where(tile < spans)
                    out_refs[c * YS + s][:, at : at + LANES] = live
                    most = live if most is None else jnp.maximum(most, live)
                    q += 1
    most = most.astype(FULL)

    @pl.when(block == 0)
    def _():
        most_ref[...] = most

    @pl.when(block > 0)
    def _():
        most_ref[...] = jnp.maximum(most_ref[...], most)


def split_counts(count_rows, lengths, here):
    steps = ZS // SPLIT
    return pl.pallas_call(
        split_kernel,
        grid_spec=pltpu.PrefetchScalarGridSpec(
            num_scalar_prefetch=1,
            grid=(steps,),
            in_specs=[
                pl.BlockSpec((1, ROWS), lambda i, y: (0, 0)),
                pl.BlockSpec((ROWS, SPLIT * YS * SHARD), lambda i, y: (0, i)),
            ],
            out_specs=[pl.BlockSpec((ROWS, LANES), lambda i, y: (0, 0))]
            + [pl.BlockSpec((ROWS, SPLIT * w), lambda i, y: (0, i)) for w in CHUNKS for _ in range(YS)],
        ),
        out_shape=[jax.ShapeDtypeStruct((ROWS, LANES), FULL)]
        + [jax.ShapeDtypeStruct((ROWS, ZS * w), HALF) for w in CHUNKS for _ in range(YS)],
        compiler_params=pltpu.CompilerParams(vmem_limit_bytes=VMEM),
        cost_estimate=pl.CostEstimate(flops=2**21, bytes_accessed=2**23, transcendentals=0),
        name="split_counts",
    )(here, lengths, count_rows)


def call(kernel, shapes, name, *args, scalars=0, after=(), passes=0):
    count = len(args)

    def body(*refs):
        kernel(*refs[:count], *refs[count + len(after) :])

    return pl.pallas_call(
        body,
        in_specs=[pl.BlockSpec(memory_space=pltpu.SMEM)] * scalars
        + [pl.BlockSpec(memory_space=pltpu.VMEM)] * (count - scalars)
        + [pl.BlockSpec(memory_space=pl.ANY)] * len(after),
        out_specs=jax.tree.map(lambda _: pl.BlockSpec(memory_space=pltpu.VMEM), shapes),
        out_shape=shapes,
        compiler_params=pltpu.CompilerParams(vmem_limit_bytes=16 * 2**20),
        cost_estimate=pl.CostEstimate(
            flops=2 * passes * GROUP * GROUP * TOPICS, bytes_accessed=2**18, transcendentals=0
        ),
        name=name,
    )(*args, *after)


def asked_column(came_ref):
    each = ones_where(iota((ROWS, TUP), 0) // EACH == iota((ROWS, TUP), 1))
    wide = jnp.dot(each, came_ref[:, :EACH].astype(FULL).astype(HALF), preferred_element_type=FULL)
    shape = (ROWS, EACH)
    picked = jnp.where(iota(shape, 0) % EACH == iota(shape, 1), wide, 0.0)
    return jnp.sum(picked, axis=1, keepdims=True).astype(jnp.int32)


def give_kernel(came_ref, topic_ref, out_ref):
    chosen = ones_where(asked_column(came_ref) == iota((ROWS, ROWS), 1))
    rows = jnp.dot(chosen, topic_ref[...], preferred_element_type=FULL).astype(HALF)
    for z in range(ZS):
        for y in range(YS):
            out_ref[z, y] = rows[z * PART : (z + 1) * PART]


def places(slot, here):
    owner = slot // PART
    behind = (here + YS - owner % YS) % YS
    return behind * ROWS + owner // YS * PART + slot % PART


def fetch_kernel(*refs):
    note_refs = refs[:YS]
    came_ref, scale_ref, arrived_ref, mix_ref, turned_ref, total_scale_ref = refs[YS:]
    level = jnp.max(came_ref[:, EACH:].astype(FULL), axis=0, keepdims=True)
    hit = iota((1, LANES), 1).astype(FULL) == level
    scale = jnp.sum(jnp.where(hit, scale_ref[...], 0.0), axis=1, keepdims=True)
    total_scale_ref[...] = jnp.broadcast_to(scale, total_scale_ref.shape)
    arrived = arrived_ref[...]
    for s in range(YS):
        chosen = ones_where(to_column(note_refs[s][...]) == iota((ROWS, GROUP), 1))
        mix = jnp.dot(chosen, arrived, preferred_element_type=FULL)
        mix_ref[s * ROWS : (s + 1) * ROWS, :] = mix.astype(HALF)
        turned_ref[:, s * ROWS : (s + 1) * ROWS] = (mix.T * scale).astype(HALF)


def pack(here, note_refs, topic, mix, out_refs):
    column = jnp.sum(topic * mix.astype(FULL), axis=0, keepdims=True)
    chosen = jnp.concatenate(
        [ones_where(places(r[...], here) == iota((GROUP, ROWS), 0)) for r in note_refs], axis=1
    )
    packed = exact_select(chosen, topic)
    for s in range(YS):
        out_refs[s][:ROWS, :] = packed[s * ROWS : (s + 1) * ROWS, :]
        out_refs[s][ROWS:, :] = jnp.broadcast_to(column, (8, TOPICS))


def join_kernel(*refs):
    out_ref = refs[YS]
    for z in range(ZS):
        rows = slice(z * PART, (z + 1) * PART)
        out_ref[z, :PART, :] = sum(r[rows, :] for r in refs[:YS])
        out_ref[z, PART:, :] = sum(r[ROWS:, :] for r in refs[:YS])


def place_kernel(came_ref, topic_ref, scale_ref, out_ref, total_ref):
    asked = to_row(asked_column(came_ref))
    chosen = ones_where(asked == iota((ROWS, ROWS), 0))
    rows = topic_ref[:, :PART, :].reshape(ROWS, TOPICS)
    out_ref[...] = exact_select(chosen, rows)
    total_ref[...] = jnp.sum(topic_ref[:, PART:, :], axis=0) * scale_ref[0:1, 0:1]


def exact_select(chosen, values):
    total = None
    rest = values
    for _ in range(3):
        piece = rest.astype(HALF)
        rest = rest - piece.astype(FULL)
        term = jnp.dot(chosen, piece, preferred_element_type=FULL)
        total = term if total is None else total + term
    return total


def trade(values, axis):
    return lax.all_to_all(values, axis, split_axis=0, concat_axis=0, tiled=True)


def shift_y(values, s):
    return lax.ppermute(values, "y", [(i, (i + s) % YS) for i in range(YS)])


def shift_z(values, s):
    return lax.ppermute(values, "z", [(i, (i + s) % ZS) for i in range(ZS)])


def ring_gather(block):
    found = {0: block}
    up = down = block
    for t in range(1, ZS // 2 + 1):
        up = found[ZS - t] = shift_z(up, 1)
        if t < ZS // 2:
            down = found[t] = shift_z(down, ZS - 1)
    return found


NEAR = (4, 5, 3, 6, 2, 7, 1, 0)
def ratio_kernel(order_ref, y_ref, *refs):
    count_refs, refs = refs[: YS * len(CHUNKS)], refs[YS * len(CHUNKS) :]
    note_refs, refs = refs[:YS], refs[YS:]
    given_refs, refs = refs[:ZS], refs[ZS:]
    mix_ref, turned_ref, refs = refs[0], refs[1], refs[2:]
    pack_refs, refs = refs[:YS], refs[YS:]
    up_ref, down_ref, rest_ref, topic_ref, word_ref, sum_ref, sems = refs
    step = pl.program_id(0)

    @pl.when(step == 0)
    def _():
        for i, ref in enumerate(given_refs):
            pltpu.make_async_copy(ref, word_ref.at[i], sems.at[i]).start()

    pltpu.make_async_copy(given_refs[0], word_ref.at[step], sems.at[step]).wait()
    mix, turned = mix_ref[...], turned_ref[...]
    words = word_ref[step]
    counts = jnp.concatenate(
        [
            jnp.concatenate([r[...] for r in count_refs[c * YS : (c + 1) * YS]], axis=0)
            for c in range(len(CHUNKS))
        ],
        axis=1,
    )
    expected = lax.dot_general(
        mix, words, (((1,), (1,)), ((), ())), preferred_element_type=FULL
    )
    ratios = counts.astype(FULL) * pl.reciprocal(expected)
    high = ratios.astype(HALF)
    low = (ratios - high.astype(FULL)).astype(HALF)
    topic = jnp.dot(
        jnp.concatenate([high, low], axis=1),
        jnp.concatenate([words, words], axis=0),
        preferred_element_type=FULL,
    )
    sum_ref[...] = jnp.dot(
        jnp.concatenate([turned, turned], axis=1),
        jnp.concatenate([high, low], axis=0),
        preferred_element_type=FULL,
    )

    @pl.when(step == 0)
    def _():
        topic_ref[...] = topic
        up_ref[...] = sum_ref[...]

    @pl.when(step > 0)
    def _():
        topic_ref[...] += topic

    @pl.when(step == 1)
    def _():
        down_ref[...] = sum_ref[...]

    @pl.when(step > 1)
    def _():
        rest_ref[0] = sum_ref[...]

    @pl.when(step == ZS - 1)
    def _():
        pack(y_ref[0], note_refs, topic_ref[...], mix, pack_refs)


def ratio_pass(parts, notes, words, mix, turned, order, here):
    def whole(*shape):
        return pl.BlockSpec(shape, lambda i, o, y: (0,) * len(shape))

    block = (TOPICS, SHARD)
    return pl.pallas_call(
        ratio_kernel,
        grid_spec=pltpu.PrefetchScalarGridSpec(
            num_scalar_prefetch=2,
            grid=(ZS,),
            in_specs=[pl.BlockSpec((ROWS, w), lambda i, o, y: (0, o[i])) for w in CHUNKS for _ in range(YS)]
            + [whole(1, ROWS)] * YS
            + [pl.BlockSpec(memory_space=pl.ANY)] * ZS
            + [whole(GROUP, TOPICS), whole(TOPICS, GROUP)],
            out_specs=[whole(ROWS + 8, TOPICS)] * YS
            + [
                whole(*block),
                whole(*block),
                pl.BlockSpec((1, *block), lambda i, o, y: (jnp.maximum(i - 2, 0), 0, 0)),
            ],
            scratch_shapes=[
                pltpu.VMEM((GROUP, TOPICS), FULL),
                pltpu.VMEM((ZS, SHARD, TOPICS), HALF),
                pltpu.VMEM(block, FULL),
                pltpu.SemaphoreType.DMA((ZS,)),
            ],
        ),
        out_shape=[jax.ShapeDtypeStruct((ROWS + 8, TOPICS), FULL)] * YS
        + [
            jax.ShapeDtypeStruct(block, FULL),
            jax.ShapeDtypeStruct(block, FULL),
            jax.ShapeDtypeStruct((ZS - 2, *block), FULL),
        ],
        compiler_params=pltpu.CompilerParams(vmem_limit_bytes=VMEM),
        cost_estimate=pl.CostEstimate(
            flops=10 * GROUP * ZS * SHARD * TOPICS,
            bytes_accessed=ZS * SHARD * (2 * GROUP + 6 * TOPICS),
            transcendentals=GROUP * ZS * SHARD,
        ),
        name="ratio_pass",
    )(order, here, *parts, *notes, *words, mix, turned)


PLACE = {near: i for i, near in enumerate(NEAR[2:])}
STRIP = 256


def ring_add(came, rest, near, zero=0.0):
    return (came.astype(FULL) + (rest[PLACE[near]] + zero)).astype(SHORT)


def zero_of(arrays):
    least = 0.0
    for a in arrays:
        least = jnp.minimum(least, jnp.abs(a[0, 0]))
    return least


def sample(*arrays):
    return sum(a[:8, :LANES].astype(FULL) for a in arrays)


def share_kernel(own_ref, part_ref, mix_ref, out_ref):
    share = ROWS // LANG
    begin = pl.multiple_of(own_ref[0] * share, share)
    mixed = mix_ref[pl.ds(begin, share), :].astype(FULL) * jnp.sum(part_ref[...], axis=0)
    update = TOPICS * mixed / jnp.sum(mixed, axis=1, keepdims=True)
    out_ref[...] = jnp.broadcast_to(update[None], out_ref.shape)


def last_kernel(sum_ref, word_ref, total_ref, out_ref):
    out_ref[0] = word_ref[...].astype(FULL) * sum_ref[...].T * (VOCAB / total_ref[0:1, :])


def last_step(sums, words, total):
    return pl.pallas_call(
        last_kernel,
        grid=(SHARD // STRIP,),
        in_specs=[
            pl.BlockSpec((TOPICS, STRIP), lambda i: (0, i)),
            pl.BlockSpec((STRIP, TOPICS), lambda i: (i, 0)),
            pl.BlockSpec((8, TOPICS), lambda i: (0, 0)),
        ],
        out_specs=pl.BlockSpec((1, STRIP, TOPICS), lambda i: (0, i, 0)),
        out_shape=jax.ShapeDtypeStruct((1, SHARD, TOPICS), FULL),
        compiler_params=pltpu.CompilerParams(vmem_limit_bytes=16 * 2**20),
        cost_estimate=pl.CostEstimate(flops=2**18, bytes_accessed=2**20, transcendentals=0),
        name="word_update",
    )(sums, words, total)


def on_device(counts, lengths, tuple_map, topic_mix, word_probs):
    here = lax.axis_index("y").astype(jnp.int32).reshape(1)
    order = (lax.axis_index("z") + jnp.array(NEAR, jnp.int32)) % ZS
    steps = jnp.asarray(np.ldexp(1.0, np.arange(LANES) - 120), FULL).reshape(1, LANES)
    scales = jnp.asarray(np.ldexp(1.0, 122 - np.arange(LANES)), FULL).reshape(1, LANES)
    most, *sent = split_counts(counts[0], lengths, here)
    parts = [
        [sent[c * YS]] + [shift_y(sent[c * YS + s], s) for s in range(1, YS)]
        for c in range(len(CHUNKS))
    ]
    note, wanted, word_local = call(
        note_kernel,
        [
            jax.ShapeDtypeStruct((1, ROWS), jnp.int32),
            jax.ShapeDtypeStruct((TUP, EACH + 1), jnp.int32),
            jax.ShapeDtypeStruct((SHARD, TOPICS), HALF),
        ],
        "note", here, tuple_map, most, steps, word_probs[0], scalars=1,
    )
    notes = [note] + [shift_y(note, s) for s in range(1, YS)]
    found = ring_gather(word_local)
    words = [found[n] for n in NEAR]
    came_ids = trade(wanted.reshape(TUP, 1, EACH + 1), ("z", "y")).reshape(TUP, EACH + 1)
    given = call(
        give_kernel, jax.ShapeDtypeStruct((ZS, YS, PART, TOPICS), HALF), "give",
        came_ids, topic_mix, after=parts[0][1:],
    )
    arrived = trade(given.reshape(TUP, PART, TOPICS), ("z", "y")).reshape(GROUP, TOPICS)
    mix, turned, scale = call(
        fetch_kernel,
        [
            jax.ShapeDtypeStruct((GROUP, TOPICS), HALF),
            jax.ShapeDtypeStruct((TOPICS, GROUP), HALF),
            jax.ShapeDtypeStruct((8, LANES), FULL),
        ],
        "fetch", *notes, came_ids, scales, arrived, after=parts[1][1:],
    )

    *packed, up, down, rest = ratio_pass(sum(parts, []), notes, words, mix, turned, order, here)
    back = [packed[0]] + [shift_y(packed[s], YS - s) for s in range(1, YS)]
    up, down = shift_z(up.astype(SHORT), 1), shift_z(down.astype(SHORT), ZS - 1)
    zero = zero_of(back[1:])
    up, down = ring_add(up, rest, 3, zero), ring_add(down, rest, 6, zero)
    joined = call(
        join_kernel, jax.ShapeDtypeStruct((ZS, PART + 8, TOPICS), FULL), "join", *back, after=[sample(up)]
    )
    came = trade(joined, "z")
    up, down = shift_z(up, 1), shift_z(down, ZS - 1)
    up, down = ring_add(up, rest, 2), ring_add(down, rest, 7)
    placed, total = call(
        place_kernel,
        [jax.ShapeDtypeStruct((ROWS, TOPICS), FULL), jax.ShapeDtypeStruct((8, TOPICS), FULL)],
        "place", came_ids, came, scale, after=[sample(up)],
    )
    share = ROWS // LANG
    shares = trade(placed.reshape(LANG, share, TOPICS), ("x", "core"))
    up, down = shift_z(up, 1), shift_z(down, ZS - 1)
    up = ring_add(up, rest, 1)
    own = (lax.axis_index("x") * CS + lax.axis_index("core")).astype(jnp.int32).reshape(1)
    update = call(
        share_kernel, jax.ShapeDtypeStruct((LANG, share, TOPICS), FULL), "share",
        own, shares, topic_mix, scalars=1, after=[sample(up)],
    )
    mix_update = trade(update, ("x", "core")).reshape(ROWS, TOPICS)
    up = shift_z(up, 1)
    sums = up.astype(FULL) + down.astype(FULL) + rest[PLACE[0]]
    return (mix_update, last_step(sums, word_probs[0], total))


def solution(mesh):
    grid = Mesh(mesh.devices.reshape(ZS, YS, XS, CS), ("z", "y", "x", "core"))
    tup, lang = ("z", "y"), ("x", "core")
    return jax.shard_map(
        on_device,
        mesh=grid,
        in_specs=(P(lang, tup, None), P(lang, tup), P(lang, tup), P(tup, None), P(lang, tup, None)),
        out_specs=(P(tup, None), P(lang, tup, None)),
        check_vma=False,
    )
```
